512 devices in a mesh: sess: 128 (over x, y, z_lo, core), blk: 4 (over z_hi).
Axes of the slice: x: 4, y: 4, z: 16 (z_hi: 4, z_lo: 4; z = z_hi * 4 + z_lo), core: 2. Of those that a mesh axis runs over, the one named last changes fastest.
Arguments:
- queries: bfloat16 [128, 64, 8192], P('sess', 'blk'), may hold values from -132 to 132
- res_cache: bfloat16 [2, 128, 1024, 1024], P(None, 'sess', 'blk'), may hold values from -6 to 6
- mig_cache: bfloat16 [2, 128, 1024, 1024], P(None, 'sess', 'blk'), may hold values from -6 to 6
- res_ids: int32 [128, 4], P('sess', 'blk'), may hold values from 0 to 3, as said below
- recv_ids: int32 [128, 4], P('sess', 'blk'), may hold values from 4 to 7, as said below
- lengths: int32 [128], P('sess'), may hold values from 320 to 2048
Outputs:
- attended: bfloat16 [128, 64, 8192], P('sess', 'blk')
The draws below stay inside these ranges and needn't reach their ends.
Inputs may be any that keep to these rules, and one draw needn't show every extreme that they name: In each session the ids of res_ids and recv_ids together are 0 to 7, each once; the first resident slots of the 4 loop members hold blocks 0 to 3 in some order. `recv_ids`: see res_ids.
All inputs are finite; a program needn't handle non-finite values.
Results may differ from the reference program's by a relative error of at most 0.01.
Values may be sent and summed in bfloat16 or wider, within the bound.
No kernel may reach another device: no remote copies, remote signals or barrier semaphores. Data moves between devices by JAX's collectives and lax.ppermute only.
A program may use at most 64 MiB of HBM per device.

```python
import math
import jax
import jax.numpy as jnp
from jax import lax

HEADS = 64
KV_HEADS = 8
HEAD = 128
BLOCK = 256
QROWS = 64
BLK_DEV = 1
MIG_DEV = 1
LOOP = 4
SESSIONS = 128
TOTAL = 8


def key_field(key):
    return jax.random.truncated_normal(key, -6.0, 6.0, (SESSIONS, LOOP * BLK_DEV * BLOCK, KV_HEADS * HEAD), jnp.float32)


def order_one(session_key):
    return jax.random.permutation(session_key, LOOP)


def session_table(session_key):
    others = jax.random.permutation(jax.random.fold_in(session_key, 1), TOTAL - LOOP - 2).astype(jnp.int32) + LOOP
    split_at = LOOP * (BLK_DEV - 1)
    if BLK_DEV > 1:
        trailing = jnp.concatenate([jnp.array([TOTAL - 2], jnp.int32), others[:split_at - 1]])
        arriving = jnp.concatenate([jnp.array([TOTAL - 1], jnp.int32), others[split_at - 1:]])
        trailing = jax.random.permutation(jax.random.fold_in(session_key, 2), trailing)
    else:
        trailing = jnp.zeros((0,), jnp.int32)
        arriving = jnp.concatenate([jnp.array([TOTAL - 2, TOTAL - 1], jnp.int32), others])
    arriving = jax.random.permutation(jax.random.fold_in(session_key, 3), arriving)
    return (trailing.astype(jnp.int32), arriving.astype(jnp.int32))


def block_table(key):
    session_keys = jax.random.split(key, SESSIONS)
    trailing, arriving = jax.vmap(session_table)(session_keys)
    first_keys = jax.random.split(jax.random.fold_in(key, 7), SESSIONS)
    firsts = jax.vmap(order_one)(first_keys).astype(jnp.int32)
    leading = firsts.reshape(SESSIONS, LOOP, 1)
    trailing = trailing.reshape(SESSIONS, LOOP, BLK_DEV - 1)
    resident = jnp.concatenate([leading, trailing], axis=2).reshape(SESSIONS, LOOP * BLK_DEV)
    arriving = arriving.reshape(SESSIONS, LOOP * MIG_DEV)
    return (resident.astype(jnp.int32), arriving.astype(jnp.int32))


def draw_res_ids(key, part):
    tables = block_table(key)
    return tables[0]


def draw_recv_ids(key, part):
    tables = block_table(key)
    return tables[1]


def draw_lengths(key, part):
    key = jax.random.fold_in(key, 3)
    lowest = BLOCK + QROWS
    highest = TOTAL * BLOCK
    drawn = jax.random.randint(jax.random.fold_in(key, 10), (SESSIONS,), lowest, highest + 1)
    spot = jax.random.randint(jax.random.fold_in(key, 11), (), 0, SESSIONS)
    drawn = drawn.at[spot].set(highest)
    drawn = drawn.at[(spot + 1) % SESSIONS].set(lowest)
    return drawn.astype(jnp.int32)


def draw_res_cache(key, part):
    keys_now = key_field(key)
    key = jax.random.fold_in(key, 4)
    values_now = jax.random.truncated_normal(key, -6.0, 6.0, keys_now.shape, jnp.float32)
    return jnp.stack([keys_now, values_now]).astype(jnp.bfloat16)


def draw_queries(key, part):
    key = jax.random.fold_in(key, 5)
    drawn = jax.random.truncated_normal(key, -6.0, 6.0, (SESSIONS, QROWS, HEADS * HEAD), jnp.float32)
    return drawn.astype(jnp.bfloat16)


def level_of(rng, extent, cuts, least, largest):
    def one(dim, shards_of):
        draws = jax.random.uniform(jax.random.fold_in(jax.random.fold_in(rng, 6), dim), (shards_of,), jnp.float32, least / len(cuts), largest / len(cuts))
        return jnp.repeat(jnp.exp(draws), extent[dim] // shards_of).reshape((-1,) + (1,) * (len(extent) - dim - 1))

    loudness = one(*cuts[0])
    for cut in cuts[1:]:
        loudness = loudness * one(*cut)
    return loudness


def normal_values(rng, shape, width, most, cuts=(), kind=jnp.bfloat16):
    values = width * jax.random.normal(rng, shape, jnp.float32)
    if cuts:
        values = values * level_of(rng, shape, cuts, -0.22, 0.18)
    return jnp.clip(values, -most, most).astype(kind)


def setup_inputs(seed: int = 0) -> dict:
    seeds = jax.random.split(jax.random.key(seed), 7)
    queries = draw_queries(jax.random.fold_in(seeds[6], 71), 0)
    res_cache = draw_res_cache(jax.random.fold_in(seeds[6], 71), 0)
    mig_cache = normal_values(seeds[2], (2, SESSIONS, LOOP * MIG_DEV * BLOCK, KV_HEADS * HEAD), 1.0, 6.0, ((1, 128), (2, 4)))
    res_ids = draw_res_ids(jax.random.fold_in(seeds[6], 71), 0)
    recv_ids = draw_recv_ids(jax.random.fold_in(seeds[6], 71), 0)
    lengths = draw_lengths(jax.random.fold_in(seeds[6], 71), 0)
    return {"queries": queries, "res_cache": res_cache, "mig_cache": mig_cache, "res_ids": res_ids, "recv_ids": recv_ids, "lengths": lengths}


def reference(queries, res_cache, mig_cache, res_ids, recv_ids, lengths):
    half_way = SESSIONS // 2
    group_size = HEADS // KV_HEADS
    scaling = 1.0 / math.sqrt(HEAD)
    offsets = jnp.arange(BLOCK, dtype=jnp.int32)

    def attend_session(session):
        partner = (session + half_way) % SESSIONS
        key_rows = jnp.concatenate([res_cache[0, session], mig_cache[0, partner]], axis=0).astype(jnp.float32)
        value_rows = jnp.concatenate([res_cache[1, session], mig_cache[1, partner]], axis=0).astype(jnp.float32)
        block_ids = jnp.concatenate([res_ids[session], recv_ids[session]], axis=0).astype(jnp.int32)
        key_pos = (block_ids[:, None] * BLOCK + offsets[None, :]).reshape(-1)
        row_pos = lengths[session] - QROWS + jnp.arange(QROWS, dtype=jnp.int32)
        query_four = queries[session].astype(jnp.float32).reshape(QROWS, KV_HEADS, group_size, HEAD)
        key_three = key_rows.reshape(-1, KV_HEADS, HEAD)
        value_three = value_rows.reshape(-1, KV_HEADS, HEAD)
        scores = jnp.einsum('rgjd,kgd->rgjk', query_four, key_three) * scaling
        allowed = (key_pos[None, :] <= row_pos[:, None])[:, None, None, :]
        row_max = lax.optimization_barrier(jnp.max(jnp.where(allowed, scores, -1e+30), axis=-1))
        weights = jnp.where(allowed, jnp.exp(scores - row_max[..., None]), 0.0).astype(jnp.bfloat16)
        weights = lax.optimization_barrier(weights).astype(jnp.float32)
        totals = lax.optimization_barrier(jnp.sum(weights, axis=-1))
        mixed_sum = jnp.einsum('rgjk,kgd->rgjd', weights, value_three)
        return (mixed_sum / totals[..., None]).reshape(QROWS, HEADS * HEAD).astype(jnp.bfloat16)
    return lax.map(attend_session, jnp.arange(SESSIONS, dtype=jnp.int32))
```

```python
import functools
import math

import jax
import jax.numpy as jnp
from jax import lax
from jax.experimental import pallas as pl
from jax.experimental.pallas import tpu as pltpu
from jax.sharding import PartitionSpec as P

HEADS = 64
KV_HEADS = 8
HEAD = 128
BLOCK = 256
QROWS = 64
GROUP = HEADS // KV_HEADS
HALF_HEADS = HEADS // 2
HALF = HALF_HEADS * HEAD
PACKET = HALF + 128
FAR = -1e30
LOG2E = math.log2(math.e)

VMEM = pl.BlockSpec(memory_space=pltpu.VMEM)
SMEM = pl.BlockSpec(memory_space=pltpu.SMEM)


def shifted(value, axis, steps):
    count = lax.axis_size(axis)
    pairs = [(source, (source + steps) % count) for source in range(count)]
    return lax.ppermute(value, axis, pairs)


def split_three(value):
    high = value.astype(jnp.bfloat16)
    rest = value - high.astype(jnp.float32)
    middle = rest.astype(jnp.bfloat16)
    low = (rest - middle.astype(jnp.float32)).astype(jnp.bfloat16)
    return high, middle, low


def put_stats(out_ref, stats):
    high, middle, low = (part.astype(jnp.float32) for part in split_three(stats))
    lane = lax.broadcasted_iota(jnp.int32, stats.shape, 1)
    middle = pltpu.roll(middle, HALF_HEADS, 1)
    low = pltpu.roll(low, 2 * HALF_HEADS, 1)
    tile = jnp.where(lane < HALF_HEADS, high, jnp.where(lane < 2 * HALF_HEADS, middle, low))
    out_ref[:, HALF:] = tile.astype(jnp.bfloat16)


def get_stats(packet_ref):
    tile = packet_ref[:, HALF:].astype(jnp.float32)
    middle = pltpu.roll(tile, 128 - HALF_HEADS, 1)
    low = pltpu.roll(tile, 128 - 2 * HALF_HEADS, 1)
    return tile + middle + low


def attend_body(jobs, info_ref, res_id_ref, recv_id_ref, length_ref, res_ref, mig_ref, *refs):
    out_refs = refs[-len(jobs):]
    query_refs = refs[: -len(jobs)]
    member = info_ref[0]
    loop = info_ref[1]
    ones = jnp.ones((2 * BLOCK, HEAD), jnp.bfloat16)
    for (distance, half, operand, first), out_ref in zip(jobs, out_refs, strict=True):
        query_ref = query_refs[operand]
        row_count = query_ref.shape[0]
        anchor = lax.rem(member + distance, loop)
        start = length_ref[0] - QROWS + anchor * row_count
        row = lax.broadcasted_iota(jnp.int32, (row_count, BLOCK), 0)
        token = lax.broadcasted_iota(jnp.int32, (row_count, BLOCK), 1)
        bias = []
        for id_ref in (res_id_ref, recv_id_ref):
            limit = start - id_ref[0, 0] * BLOCK
            bias.append(jnp.where(token <= row + limit, 0.0, FAR).astype(jnp.float32))
        bias = jnp.concatenate(bias, axis=1)
        bias = jnp.concatenate([bias] * GROUP, axis=0)
        lane = lax.broadcasted_iota(jnp.int32, (row_count, 128), 1)
        stats = jnp.zeros((row_count, 128), jnp.float32)
        for local in range(KV_HEADS // 2):
            kv_head = half * (KV_HEADS // 2) + local
            columns = slice(kv_head * HEAD, (kv_head + 1) * HEAD)
            query = jnp.concatenate(
                [
                    query_ref[:, first + (local * GROUP + j) * HEAD : first + (local * GROUP + j + 1) * HEAD]
                    for j in range(GROUP)
                ],
                axis=0,
            )
            keys = jnp.concatenate([res_ref[0, 0, :, columns], mig_ref[0, 0, :, columns]], axis=0)
            values = jnp.concatenate([res_ref[1, 0, :, columns], mig_ref[1, 0, :, columns]], axis=0)
            scores = lax.dot_general(
                query, keys, (((1,), (1,)), ((), ())), preferred_element_type=jnp.float32
            )
            scores = scores * (LOG2E / math.sqrt(HEAD)) + bias
            row_max = jnp.max(scores, axis=1, keepdims=True)
            weights = jnp.exp2(scores - row_max).astype(jnp.bfloat16)
            mixed = jnp.dot(
                weights,
                jnp.concatenate([values, ones], axis=1),
                preferred_element_type=jnp.float32,
            )
            totals = mixed[:, HEAD:]
            scaled = (mixed[:, :HEAD] / totals).astype(jnp.bfloat16)
            level = row_max + jnp.log2(totals)
            for j in range(GROUP):
                head = local * GROUP + j
                rows = slice(j * row_count, (j + 1) * row_count)
                out_ref[:, head * HEAD : (head + 1) * HEAD] = scaled[rows]
                stats = jnp.where(lane == head, level[rows], stats)
        put_stats(out_ref, stats)


def attend(info, ids, res_cache, mig_cache, queries, jobs, name):
    row_count = queries[0].shape[0]
    packet = jax.ShapeDtypeStruct((row_count, PACKET), jnp.bfloat16)
    pairs = len(jobs) * row_count * HALF_HEADS * 2 * BLOCK
    return pl.pallas_call(
        functools.partial(attend_body, jobs),
        out_shape=[packet] * len(jobs),
        in_specs=[SMEM] * 4 + [VMEM] * (2 + len(queries)),
        out_specs=[VMEM] * len(jobs),
        compiler_params=pltpu.CompilerParams(vmem_limit_bytes=32 * 1024 * 1024),
        cost_estimate=pl.CostEstimate(
            flops=pairs * HEAD * 4, bytes_accessed=2 * 1024 * 1024, transcendentals=pairs
        ),
        name=name,
    )(info, *ids, res_cache, mig_cache, *queries)


def join_body(groups, width, *refs):
    in_refs = refs[: sum(groups)]
    out_refs = refs[sum(groups):]
    at = 0
    for index, size in enumerate(groups):
        packets = in_refs[at : at + size]
        at += size
        stats = [get_stats(packet) for packet in packets]
        top = functools.reduce(jnp.maximum, stats)
        shares = [jnp.exp2(stat - top) for stat in stats]
        total = functools.reduce(jnp.add, shares)
        shares = [share / total for share in shares]
        out_ref = out_refs[0] if width else out_refs[index]
        shift = index * HALF if width else 0
        for head in range(HALF_HEADS):
            columns = slice(head * HEAD, (head + 1) * HEAD)
            joined = functools.reduce(
                jnp.add,
                [
                    packet[:, columns].astype(jnp.float32) * share[:, head : head + 1]
                    for packet, share in zip(packets, shares, strict=True)
                ],
            )
            out_ref[:, shift + head * HEAD : shift + (head + 1) * HEAD] = joined.astype(jnp.bfloat16)
        if not width:
            lane = lax.broadcasted_iota(jnp.int32, top.shape, 1)
            put_stats(out_ref, jnp.where(lane < HALF_HEADS, top + jnp.log2(total), 0.0))


def join(groups, name, width=0):
    row_count = groups[0][0].shape[0]
    if width:
        shape = jax.ShapeDtypeStruct((row_count, width), jnp.bfloat16)
    else:
        shape = [jax.ShapeDtypeStruct((row_count, PACKET), jnp.bfloat16)] * len(groups)
    packets = [packet for group in groups for packet in group]
    return pl.pallas_call(
        functools.partial(join_body, tuple(len(group) for group in groups), width),
        out_shape=shape,
        in_specs=[VMEM] * len(packets),
        out_specs=VMEM if width else [VMEM] * len(groups),
        compiler_params=pltpu.CompilerParams(vmem_limit_bytes=32 * 1024 * 1024),
        cost_estimate=pl.CostEstimate(
            flops=len(packets) * row_count * HALF * 2,
            bytes_accessed=len(packets) * row_count * PACKET * 2,
            transcendentals=0,
        ),
        name=name,
    )(*packets)


def per_device(queries, res_cache, mig_cache, res_ids, recv_ids, lengths):
    loop = lax.axis_size("blk")
    info = jnp.stack([lax.axis_index("blk"), jnp.int32(loop)]).astype(jnp.int32)
    ids = (res_ids, recv_ids, lengths)
    mine = queries[0]
    mine_a, mine_b = mine[:, :HALF], mine[:, HALF:]

    arrived = shifted(mig_cache, "sess", lax.axis_size("sess") // 2)
    left_a = shifted(mine_a, "blk", 1)
    right_b = shifted(mine_b, "blk", -1)
    left_b = shifted(mine_b, "blk", 1)
    right_a = shifted(mine_a, "blk", -1)
    far_a = shifted(left_a, "blk", 1)
    far_b = shifted(right_b, "blk", -1)

    run = functools.partial(attend, info, ids, res_cache, arrived)
    to_right_b, to_left_a = run(
        (right_b, left_a), ((1, 1, 0, 0), (loop - 1, 0, 1, 0)), "near_direct"
    )
    from_left_b = shifted(to_right_b, "blk", 1)
    from_right_a = shifted(to_left_a, "blk", -1)
    to_right_a, to_left_b = run(
        (right_a, left_b), ((1, 0, 0, 0), (loop - 1, 1, 1, 0)), "near_joined"
    )
    far_out_a, far_out_b = run((far_a, far_b), ((2, 0, 0, 0), (2, 1, 1, 0)), "far")
    via_left_a = shifted(far_out_a, "blk", 1)
    via_right_b = shifted(far_out_b, "blk", -1)
    own_a, own_b = run((mine,), ((0, 0, 0, 0), (0, 1, 0, HALF)), "own")
    (sum_right_a,) = join(((to_right_a, via_left_a),), "join_right")
    from_left_a = shifted(sum_right_a, "blk", 1)
    (sum_left_b,) = join(((to_left_b, via_right_b),), "join_left")
    from_right_b = shifted(sum_left_b, "blk", -1)
    out = join(
        ((own_a, from_right_a, from_left_a), (own_b, from_left_b, from_right_b)),
        "join_home",
        2 * HALF,
    )
    return out[None]


def solution(mesh):
    placed = (
        P("sess", "blk", None),
        P(None, "sess", "blk", None),
        P(None, "sess", "blk", None),
        P("sess", "blk"),
        P("sess", "blk"),
        P("sess"),
    )
    return jax.shard_map(
        per_device, mesh=mesh, in_specs=placed, out_specs=P("sess", "blk", None), check_vma=False
    )
```

```python
import functools
import math

import jax
import jax.numpy as jnp
from jax import lax
from jax.experimental import pallas as pl
from jax.experimental.pallas import tpu as pltpu
from jax.sharding import PartitionSpec as P

HEADS = 64
KV_HEADS = 8
HEAD = 128
BLOCK = 256
QROWS = 64
GROUP = HEADS // KV_HEADS
HALF_HEADS = HEADS // 2
HALF = HALF_HEADS * HEAD
PACKET = HALF + 128
FAR = -1e30
LOG2E = math.log2(math.e)

VMEM = pl.BlockSpec(memory_space=pltpu.VMEM)
SMEM = pl.BlockSpec(memory_space=pltpu.SMEM)


def shifted(value, axis, steps):
    count = lax.axis_size(axis)
    pairs = [(source, (source + steps) % count) for source in range(count)]
    return lax.ppermute(value, axis, pairs)


def split_three(value):
    high = value.astype(jnp.bfloat16)
    rest = value - high.astype(jnp.float32)
    middle = rest.astype(jnp.bfloat16)
    low = (rest - middle.astype(jnp.float32)).astype(jnp.bfloat16)
    return high, middle, low


def put_stats(out_ref, stats):
    high, middle, low = (part.astype(jnp.float32) for part in split_three(stats))
    lane = lax.broadcasted_iota(jnp.int32, stats.shape, 1)
    middle = pltpu.roll(middle, HALF_HEADS, 1)
    low = pltpu.roll(low, 2 * HALF_HEADS, 1)
    tile = jnp.where(lane < HALF_HEADS, high, jnp.where(lane < 2 * HALF_HEADS, middle, low))
    out_ref[:, HALF:] = tile.astype(jnp.bfloat16)


def get_stats(packet_ref):
    tile = packet_ref[:, HALF:].astype(jnp.float32)
    middle = pltpu.roll(tile, 128 - HALF_HEADS, 1)
    low = pltpu.roll(tile, 128 - 2 * HALF_HEADS, 1)
    return tile + middle + low


def attend_body(loop, distance, info_ref, res_id_ref, recv_id_ref, length_ref, query_ref, res_ref, mig_ref, *out_refs):
    row_count = query_ref.shape[0]
    anchor = lax.rem(info_ref[0] + distance * info_ref[1], loop)
    start = length_ref[0] - QROWS + anchor * row_count
    row = lax.broadcasted_iota(jnp.int32, (row_count, BLOCK), 0)
    token = lax.broadcasted_iota(jnp.int32, (row_count, BLOCK), 1)
    bias = []
    for id_ref in (res_id_ref, recv_id_ref):
        limit = start - id_ref[0, 0] * BLOCK
        bias.append(jnp.where(token <= row + limit, 0.0, FAR).astype(jnp.float32))
    bias = jnp.concatenate(bias, axis=1)
    bias = jnp.concatenate([bias] * GROUP, axis=0)
    ones = jnp.ones((2 * BLOCK, HEAD), jnp.bfloat16)
    lane = lax.broadcasted_iota(jnp.int32, (row_count, 128), 1)
    for half, out_ref in enumerate(out_refs):
        stats = jnp.zeros((row_count, 128), jnp.float32)
        for local in range(KV_HEADS // 2):
            kv_head = half * (KV_HEADS // 2) + local
            columns = slice(kv_head * HEAD, (kv_head + 1) * HEAD)
            heads = [kv_head * GROUP + j for j in range(GROUP)]
            query = jnp.concatenate([query_ref[:, h * HEAD : (h + 1) * HEAD] for h in heads], axis=0)
            keys = jnp.concatenate([res_ref[0, 0, :, columns], mig_ref[0, 0, :, columns]], axis=0)
            values = jnp.concatenate([res_ref[1, 0, :, columns], mig_ref[1, 0, :, columns]], axis=0)
            scores = lax.dot_general(
                query, keys, (((1,), (1,)), ((), ())), preferred_element_type=jnp.float32
            )
            scores = scores * (LOG2E / math.sqrt(HEAD)) + bias
            row_max = jnp.max(scores, axis=1, keepdims=True)
            weights = jnp.exp2(scores - row_max).astype(jnp.bfloat16)
            mixed = jnp.dot(
                weights,
                jnp.concatenate([values, ones], axis=1),
                preferred_element_type=jnp.float32,
            )
            totals = mixed[:, HEAD:]
            scaled = (mixed[:, :HEAD] / totals).astype(jnp.bfloat16)
            level = row_max + jnp.log2(totals)
            for j in range(GROUP):
                head = local * GROUP + j
                rows = slice(j * row_count, (j + 1) * row_count)
                out_ref[:, head * HEAD : (head + 1) * HEAD] = scaled[rows]
                stats = jnp.where(lane == head, level[rows], stats)
        put_stats(out_ref, stats)


def whole_body(loop, distance, *refs):
    out_ref = refs[-1]
    halves = [out_ref.at[:, half * PACKET : (half + 1) * PACKET] for half in range(2)]
    attend_body(loop, distance, *refs[:-1], *halves)


def attend(loop, info, ids, res_cache, mig_cache, queries, distance, name, split=False):
    row_count = queries.shape[0]
    pairs = row_count * HEADS * 2 * BLOCK
    packet = jax.ShapeDtypeStruct((row_count, PACKET), jnp.bfloat16)
    return pl.pallas_call(
        functools.partial(attend_body if split else whole_body, loop, distance),
        out_shape=[packet] * 2 if split else jax.ShapeDtypeStruct((row_count, 2 * PACKET), jnp.bfloat16),
        in_specs=[SMEM] * 4 + [VMEM] * 3,
        out_specs=[VMEM] * 2 if split else VMEM,
        compiler_params=pltpu.CompilerParams(vmem_limit_bytes=32 * 1024 * 1024),
        cost_estimate=pl.CostEstimate(
            flops=pairs * HEAD * 4, bytes_accessed=2 * 1024 * 1024, transcendentals=pairs
        ),
        name=name,
    )(info, *ids, queries, res_cache, mig_cache)


def join_packets(packets):
    stats = [get_stats(packet) for packet in packets]
    top = functools.reduce(jnp.maximum, stats)
    shares = [jnp.exp2(stat - top) for stat in stats]
    total = functools.reduce(jnp.add, shares)
    heads = []
    for head in range(HALF_HEADS):
        columns = slice(head * HEAD, (head + 1) * HEAD)
        parts = [
            packet[:, columns].astype(jnp.float32) * (share / total)[:, head : head + 1]
            for packet, share in zip(packets, shares, strict=True)
        ]
        heads.append(functools.reduce(jnp.add, parts))
    return heads, top + jnp.log2(total)


def join_body(*refs):
    out_ref = refs[-1]
    heads, stats = join_packets(refs[:-1])
    for head, joined in enumerate(heads):
        out_ref[:, head * HEAD : (head + 1) * HEAD] = joined.astype(jnp.bfloat16)
    lane = lax.broadcasted_iota(jnp.int32, stats.shape, 1)
    put_stats(out_ref, jnp.where(lane < HALF_HEADS, stats, 0.0))


def join_home_body(own_ref, direct_ref, summed_a_ref, summed_b_ref, out_ref):
    for half, summed_ref in enumerate((summed_a_ref, summed_b_ref)):
        part = slice(half * PACKET, (half + 1) * PACKET)
        heads, _ = join_packets([own_ref.at[:, part], direct_ref.at[:, part], summed_ref])
        for head, joined in enumerate(heads):
            first = half * HALF + head * HEAD
            out_ref[:, first : first + HEAD] = joined.astype(jnp.bfloat16)


def join_call(body, packets, columns, name):
    row_count = packets[0].shape[0]
    return pl.pallas_call(
        body,
        out_shape=jax.ShapeDtypeStruct((row_count, columns), jnp.bfloat16),
        in_specs=[VMEM] * len(packets),
        out_specs=VMEM,
        compiler_params=pltpu.CompilerParams(vmem_limit_bytes=32 * 1024 * 1024),
        cost_estimate=pl.CostEstimate(
            flops=len(packets) * row_count * HALF * 2,
            bytes_accessed=len(packets) * row_count * PACKET * 2,
            transcendentals=0,
        ),
        name=name,
    )(*packets)


def join(packets, name):
    return join_call(join_body, packets, PACKET, name)


def join_home(own, direct, summed):
    return join_call(join_home_body, (own, direct, *summed), 2 * HALF, "join_home")


def along(value, steps):
    sessions, loop = lax.axis_size("sess"), lax.axis_size("blk")
    pairs = [
        (s * loop + b, s * loop + (b + (steps if s % 2 == 0 else -steps)) % loop)
        for s in range(sessions)
        for b in range(loop)
    ]
    return lax.ppermute(value, ("sess", "blk"), pairs)


def per_device(queries, res_cache, mig_cache, res_ids, recv_ids, lengths):
    loop = lax.axis_size("blk")
    way = 1 - 2 * lax.rem(lax.axis_index("sess"), 2)
    info = jnp.stack([lax.axis_index("blk") + loop, way]).astype(jnp.int32)
    ids = (res_ids, recv_ids, lengths)
    mine = queries[0]

    before = along(mine, 1)
    arrived = shifted(mig_cache, "sess", lax.axis_size("sess") // 2)
    after = along(mine, -1)
    far = along(before, 1)

    run = functools.partial(attend, loop, info, ids, res_cache, arrived)
    home_1 = along(run(before, -1, "attend_before"), -1)
    after_a, after_b = run(after, 1, "attend_after", split=True)
    far, after_a, after_b = lax.optimization_barrier((far, after_a, after_b))
    far_a, far_b = run(far, 2, "attend_far", split=True)
    via_a = along(far_a, 1)
    via_b = along(far_b, 1)
    mine, home_1 = lax.optimization_barrier((mine, home_1))
    own = run(mine, 0, "attend_own")
    after_a, own = lax.optimization_barrier((after_a, own))
    home_2a = along(join((after_a, via_a), "join_a"), 1)
    home_2b = along(join((after_b, via_b), "join_b"), 1)
    return join_home(own, home_1, (home_2a, home_2b))[None]


def solution(mesh):
    placed = (
        P("sess", "blk", None),
        P(None, "sess", "blk", None),
        P(None, "sess", "blk", None),
        P("sess", "blk"),
        P("sess", "blk"),
        P("sess"),
    )
    return jax.shard_map(
        per_device, mesh=mesh, in_specs=placed, out_specs=P("sess", "blk", None), check_vma=False
    )
```

```python
import functools
import math

import jax
import jax.numpy as jnp
from jax import lax
from jax.experimental import pallas as pl
from jax.experimental.pallas import tpu as pltpu
from jax.sharding import PartitionSpec as P

HEADS = 64
KV_HEADS = 8
HEAD = 128
BLOCK = 256
QROWS = 64
GROUP = HEADS // KV_HEADS
TILE = 128
PARTS = ((0, KV_HEADS // 2), (KV_HEADS // 2, KV_HEADS))
FAR = -1e30
LOG2E = math.log2(math.e)

VMEM = pl.BlockSpec(memory_space=pltpu.VMEM)
SMEM = pl.BlockSpec(memory_space=pltpu.SMEM)


def shifted(value, axis, steps):
    count = lax.axis_size(axis)
    pairs = [(source, (source + steps) % count) for source in range(count)]
    return lax.ppermute(value, axis, pairs)


def split_three(value):
    high = value.astype(jnp.bfloat16)
    rest = value - high.astype(jnp.float32)
    middle = rest.astype(jnp.bfloat16)
    low = (rest - middle.astype(jnp.float32)).astype(jnp.bfloat16)
    return high, middle, low


def packet_heads(packet):
    return (packet.shape[1] - TILE) // HEAD


def put_stats(out_ref, stats):
    heads = packet_heads(out_ref)
    high, middle, low = (term.astype(jnp.float32) for term in split_three(stats))
    lane = lax.broadcasted_iota(jnp.int32, stats.shape, 1)
    middle = pltpu.roll(middle, heads, 1)
    low = pltpu.roll(low, 2 * heads, 1)
    tile = jnp.where(lane < heads, high, jnp.where(lane < 2 * heads, middle, low))
    out_ref[:, heads * HEAD :] = tile.astype(jnp.bfloat16)


def get_stats(packet_ref):
    heads = packet_heads(packet_ref)
    tile = packet_ref[:, heads * HEAD :].astype(jnp.float32)
    middle = pltpu.roll(tile, TILE - heads, 1)
    low = pltpu.roll(tile, TILE - 2 * heads, 1)
    return tile + middle + low


def sections(ref):
    width = GROUP * HEAD
    return [
        ref.at[:, first * width + part * TILE : last * width + (part + 1) * TILE]
        for part, (first, last) in enumerate(PARTS)
    ]


def attend_body(loop, distance, counts, info_ref, res_id_ref, recv_id_ref, length_ref, res_ref, mig_ref, *refs):
    query_counts, packet_counts, forward, base = counts
    query_refs = refs[: len(query_counts)]
    out_refs = refs[len(query_counts) :]
    packet_refs = sections(out_refs[0]) if out_refs[0].shape[1] > HEADS * HEAD else out_refs
    row_count = query_refs[0].shape[0]
    anchor = lax.rem(info_ref[0] + distance * info_ref[1], loop)
    start = length_ref[0] - QROWS + anchor * row_count
    row = lax.broadcasted_iota(jnp.int32, (row_count, BLOCK), 0)
    token = lax.broadcasted_iota(jnp.int32, (row_count, BLOCK), 1)
    bias = []
    for id_ref in (res_id_ref, recv_id_ref):
        limit = start - id_ref[0, 0] * BLOCK
        bias.append(jnp.where(token <= row + limit, 0.0, FAR).astype(jnp.float32))
    bias = jnp.concatenate(bias, axis=1)
    bias = jnp.concatenate([bias] * GROUP, axis=0)
    ones = jnp.ones((2 * BLOCK, HEAD), jnp.bfloat16)
    lane = lax.broadcasted_iota(jnp.int32, (row_count, TILE), 1)
    if forward:
        at = 0
        for query_ref in query_refs:
            out_refs[-1][:, at : at + query_ref.shape[1]] = query_ref[...]
            at += query_ref.shape[1]
    sources = [(ref, local) for ref, count in zip(query_refs, query_counts, strict=True) for local in range(count)]
    key_head = base
    for out_ref, count in zip(packet_refs, packet_counts):
        stats = jnp.zeros((row_count, TILE), jnp.float32)
        for local in range(count):
            query_ref, place = sources[key_head - base]
            columns = slice(key_head * HEAD, (key_head + 1) * HEAD)
            key_head += 1
            query = jnp.concatenate(
                [
                    query_ref[:, (place * GROUP + j) * HEAD : (place * GROUP + j + 1) * HEAD]
                    for j in range(GROUP)
                ],
                axis=0,
            )
            keys = jnp.concatenate([res_ref[0, 0, :, columns], mig_ref[0, 0, :, columns]], axis=0)
            values = jnp.concatenate([res_ref[1, 0, :, columns], mig_ref[1, 0, :, columns]], axis=0)
            scores = lax.dot_general(
                query, keys, (((1,), (1,)), ((), ())), preferred_element_type=jnp.float32
            )
            scores = scores * (LOG2E / math.sqrt(HEAD)) + bias
            row_max = jnp.max(scores, axis=1, keepdims=True)
            weights = jnp.exp2(scores - row_max).astype(jnp.bfloat16)
            mixed = jnp.dot(
                weights,
                jnp.concatenate([values, ones], axis=1),
                preferred_element_type=jnp.float32,
            )
            totals = mixed[:, HEAD:]
            scaled = (mixed[:, :HEAD] / totals).astype(jnp.bfloat16)
            level = row_max + jnp.log2(totals)
            for j in range(GROUP):
                head = local * GROUP + j
                rows = slice(j * row_count, (j + 1) * row_count)
                out_ref[:, head * HEAD : (head + 1) * HEAD] = scaled[rows]
                stats = jnp.where(lane == head, level[rows], stats)
        put_stats(out_ref, stats)


def call(body, operands, columns, scalars, cost, name):
    row_count = operands[-1].shape[0]
    flops, loaded, transcendentals = cost
    return pl.pallas_call(
        body,
        out_shape=[jax.ShapeDtypeStruct((row_count, width), jnp.bfloat16) for width in columns],
        in_specs=[SMEM] * scalars + [VMEM] * (len(operands) - scalars),
        out_specs=[VMEM] * len(columns),
        compiler_params=pltpu.CompilerParams(vmem_limit_bytes=16 * 1024 * 1024),
        cost_estimate=pl.CostEstimate(
            flops=flops, bytes_accessed=loaded, transcendentals=transcendentals
        ),
        name=name,
    )(*operands)


def attend(loop, scalars, res_cache, mig_cache, queries, distance, name, forward=False, single=False, parts=(0, 1)):
    width = GROUP * HEAD
    query_counts = tuple(part.shape[1] // width for part in queries)
    packet_counts = tuple(PARTS[part][1] - PARTS[part][0] for part in parts)
    columns = [count * width + TILE for count in packet_counts]
    columns = ([sum(columns)] if single else columns) + [KV_HEADS * width] * forward
    pairs = queries[0].shape[0] * sum(query_counts) * GROUP * 2 * BLOCK
    return call(
        functools.partial(attend_body, loop, distance, (query_counts, packet_counts, forward, PARTS[parts[0]][0])),
        (*scalars, res_cache, mig_cache, *queries),
        columns,
        len(scalars),
        (pairs * HEAD * 4, 2 * 1024 * 1024, pairs),
        name,
    )


def join_packets(packets):
    stats = [get_stats(packet) for packet in packets]
    top = functools.reduce(jnp.maximum, stats)
    shares = [jnp.exp2(stat - top) for stat in stats]
    total = functools.reduce(jnp.add, shares)
    shares = [share / total for share in shares]
    heads = []
    for head in range(packet_heads(packets[0])):
        columns = slice(head * HEAD, (head + 1) * HEAD)
        terms = [
            packet[:, columns].astype(jnp.float32) * share[:, head : head + 1]
            for packet, share in zip(packets, shares, strict=True)
        ]
        heads.append(functools.reduce(jnp.add, terms))
    return heads, top + jnp.log2(total)


def put_heads(out_ref, first, heads):
    for head, joined in enumerate(heads, first):
        out_ref[:, head * HEAD : (head + 1) * HEAD] = joined.astype(jnp.bfloat16)


def join_body(*refs):
    count = len(refs) // 2
    ones, others, outs = refs[:count], refs[count : len(refs) - count], refs[len(refs) - count :]
    if len(others) < count:
        others = sections(others[0])
    for one_ref, other_ref, out_ref in zip(ones, others, outs, strict=True):
        heads, stats = join_packets((one_ref, other_ref))
        put_heads(out_ref, 0, heads)
        lane = lax.broadcasted_iota(jnp.int32, stats.shape, 1)
        put_stats(out_ref, jnp.where(lane < len(heads), stats, 0.0))


def join_part_body(own_ref, sum_ref, out_ref):
    put_heads(out_ref, 0, join_packets((own_ref, sum_ref))[0])


def join_home_body(done_ref, own_ref, sum_ref, out_ref):
    out_ref[:, : done_ref.shape[1]] = done_ref[...]
    put_heads(out_ref, done_ref.shape[1] // HEAD, join_packets((own_ref, sum_ref))[0])


def join(body, operands, columns, name):
    size = operands[0].shape[0] * sum(columns)
    return call(body, operands, columns, 0, (4 * size, 6 * size, 0), name)


def join_sums(ones, others, name):
    return join(join_body, (*ones, *others), [one.shape[1] for one in ones], name)


def join_home(own, sums):
    (part,) = join(join_part_body, (own[0], sums[0]), [own[0].shape[1] - TILE], "join_part")
    (whole,) = join(join_home_body, (part, own[1], sums[1]), [HEADS * HEAD], "join_home")
    return whole


def onward(value):
    sessions, loop = lax.axis_size("sess"), lax.axis_size("blk")
    pairs = [
        (s * loop + b, s * loop + (b + (1 if s % 2 == 0 else -1)) % loop)
        for s in range(sessions)
        for b in range(loop)
    ]
    return lax.ppermute(value, ("sess", "blk"), pairs)


def per_device(queries, res_cache, mig_cache, res_ids, recv_ids, lengths):
    loop = lax.axis_size("blk")
    way = 1 - 2 * lax.rem(lax.axis_index("sess"), 2)
    info = jnp.stack([lax.axis_index("blk") + loop, way]).astype(jnp.int32)
    scalars = (info, res_ids, recv_ids, lengths)
    mine = queries[0]
    mine = tuple(
        mine[:, first * GROUP * HEAD : last * GROUP * HEAD] for first, last in PARTS
    )
    arrived = shifted(mig_cache, "sess", lax.axis_size("sess") // 2)
    run = functools.partial(attend, loop, scalars, res_cache, arrived)
    before = tuple(onward(part) for part in mine)
    far_a, far_b = tuple(onward(part) for part in before)
    first_a, first_b = tuple(onward(part) for part in run(before, -1, "attend_before"))
    after_a = onward(far_a)
    part_far = run((far_a, far_b), -2, "attend_far")
    (sum_a,) = join_sums(part_far[:1], (first_a,), "join_far_a")
    second_a = onward(sum_a)
    far_b, sum_a = lax.optimization_barrier((far_b, sum_a))
    after_b = onward(far_b)
    (sum_b,) = join_sums(part_far[1:], (first_b,), "join_far_b")
    second_b = onward(sum_b)
    after_a, sum_b = lax.optimization_barrier((after_a, sum_b))
    (sum_a,) = join_sums(run((after_a,), 1, "attend_after_a", parts=(0,)), (second_a,), "join_after_a")
    third_a = onward(sum_a)
    after_b, sum_a = lax.optimization_barrier((after_b, sum_a))
    (sum_b,) = join_sums(run((after_b,), 1, "attend_after_b", parts=(1,)), (second_b,), "join_after_b")
    third_b = onward(sum_b)
    mine, third_a = lax.optimization_barrier((mine, third_a))
    own = run(mine, 0, "attend_own")
    return join_home(own, (third_a, third_b))[None]


def solution(mesh):
    placed = (
        P("sess", "blk", None),
        P(None, "sess", "blk", None),
        P(None, "sess", "blk", None),
        P("sess", "blk"),
        P("sess", "blk"),
        P("sess"),
    )
    return jax.shard_map(
        per_device, mesh=mesh, in_specs=placed, out_specs=P("sess", "blk", None), check_vma=False
    )
```

```python
import functools
import math

import jax
import jax.numpy as jnp
from jax import lax
from jax.experimental import pallas as pl
from jax.experimental.pallas import tpu as pltpu
from jax.sharding import PartitionSpec as P

HEADS = 64
KV_HEADS = 8
HEAD = 128
BLOCK = 256
QROWS = 64
GROUP = HEADS // KV_HEADS
TILE = 128
PARTS = ((0, KV_HEADS // 2), (KV_HEADS // 2, KV_HEADS))
FAR = -1e30
LOG2E = math.log2(math.e)

VMEM = pl.BlockSpec(memory_space=pltpu.VMEM)
SMEM = pl.BlockSpec(memory_space=pltpu.SMEM)


def half_way(value):
    count = lax.axis_size("sess")
    return lax.ppermute(value, "sess", [(s, (s + count // 2) % count) for s in range(count)])


def load_body(in_ref, out_ref, sem):
    copy = pltpu.make_async_copy(in_ref, out_ref, sem)
    copy.start()
    copy.wait()


def load(value):
    return pl.pallas_call(
        load_body,
        out_shape=jax.ShapeDtypeStruct(value.shape, value.dtype),
        in_specs=[pl.BlockSpec(memory_space=pl.ANY)],
        out_specs=VMEM,
        scratch_shapes=[pltpu.SemaphoreType.DMA],
        compiler_params=pltpu.CompilerParams(vmem_limit_bytes=16 * 1024 * 1024),
        cost_estimate=pl.CostEstimate(flops=0, bytes_accessed=2 * value.size * 2, transcendentals=0),
        name="load",
    )(value)


def split_three(value):
    high = value.astype(jnp.bfloat16)
    rest = value - high.astype(jnp.float32)
    middle = rest.astype(jnp.bfloat16)
    low = (rest - middle.astype(jnp.float32)).astype(jnp.bfloat16)
    return high, middle, low


def packet_heads(packet):
    return (packet.shape[1] - TILE) // HEAD


def put_stats(out_ref, stats):
    heads = packet_heads(out_ref)
    high, middle, low = (term.astype(jnp.float32) for term in split_three(stats))
    lane = lax.broadcasted_iota(jnp.int32, stats.shape, 1)
    middle = pltpu.roll(middle, heads, 1)
    low = pltpu.roll(low, 2 * heads, 1)
    tile = jnp.where(lane < heads, high, jnp.where(lane < 2 * heads, middle, low))
    out_ref[:, heads * HEAD :] = tile.astype(jnp.bfloat16)


def get_stats(packet_ref):
    heads = packet_heads(packet_ref)
    tile = packet_ref[:, heads * HEAD :].astype(jnp.float32)
    middle = pltpu.roll(tile, TILE - heads, 1)
    low = pltpu.roll(tile, TILE - 2 * heads, 1)
    return tile + middle + low


def sections(ref):
    width = GROUP * HEAD
    return [
        ref.at[:, first * width + part * TILE : last * width + (part + 1) * TILE]
        for part, (first, last) in enumerate(PARTS)
    ]


def attend_body(loop, distance, counts, res_id_ref, recv_id_ref, length_ref, res_ref, mig_ref, *refs):
    query_counts, packet_counts, forward, base = counts
    query_refs = refs[: len(query_counts)]
    out_refs = refs[len(query_counts) :]
    packet_refs = sections(out_refs[0]) if out_refs[0].shape[1] > HEADS * HEAD else out_refs
    row_count = query_refs[0].shape[0]
    way = 2 * lax.rem(lax.div(lax.axis_index("sess"), 2), 2) - 1
    anchor = lax.rem(lax.axis_index("blk") + loop + distance * way, loop)
    start = length_ref[0] - QROWS + anchor * row_count
    row = lax.broadcasted_iota(jnp.int32, (row_count, BLOCK), 0)
    token = lax.broadcasted_iota(jnp.int32, (row_count, BLOCK), 1)
    bias = []
    for id_ref in (res_id_ref, recv_id_ref):
        limit = start - id_ref[0, 0] * BLOCK
        bias.append(jnp.where(token <= row + limit, 0.0, FAR).astype(jnp.float32))
    bias = jnp.concatenate(bias, axis=1)
    bias = jnp.concatenate([bias] * GROUP, axis=0)
    ones = jnp.ones((2 * BLOCK, HEAD), jnp.bfloat16)
    lane = lax.broadcasted_iota(jnp.int32, (row_count, TILE), 1)
    if forward:
        at = 0
        for query_ref in query_refs:
            out_refs[-1][:, at : at + query_ref.shape[1]] = query_ref[...]
            at += query_ref.shape[1]
    sources = [(ref, local) for ref, count in zip(query_refs, query_counts, strict=True) for local in range(count)]
    key_head = base
    for out_ref, count in zip(packet_refs, packet_counts):
        stats = jnp.zeros((row_count, TILE), jnp.float32)
        for local in range(count):
            query_ref, place = sources[key_head - base]
            columns = slice(key_head * HEAD, (key_head + 1) * HEAD)
            key_head += 1
            query = jnp.concatenate(
                [
                    query_ref[:, (place * GROUP + j) * HEAD : (place * GROUP + j + 1) * HEAD]
                    for j in range(GROUP)
                ],
                axis=0,
            )
            keys = jnp.concatenate([res_ref[0, 0, :, columns], mig_ref[0, 0, :, columns]], axis=0)
            values = jnp.concatenate([res_ref[1, 0, :, columns], mig_ref[1, 0, :, columns]], axis=0)
            scores = lax.dot_general(
                query, keys, (((1,), (1,)), ((), ())), preferred_element_type=jnp.float32
            )
            scores = scores * (LOG2E / math.sqrt(HEAD)) + bias
            row_max = jnp.max(scores, axis=1, keepdims=True)
            weights = jnp.exp2(scores - row_max).astype(jnp.bfloat16)
            mixed = jnp.dot(
                weights,
                jnp.concatenate([values, ones], axis=1),
                preferred_element_type=jnp.float32,
            )
            totals = mixed[:, HEAD:]
            scaled = (mixed[:, :HEAD] / totals).astype(jnp.bfloat16)
            level = row_max + jnp.log2(totals)
            for j in range(GROUP):
                head = local * GROUP + j
                rows = slice(j * row_count, (j + 1) * row_count)
                out_ref[:, head * HEAD : (head + 1) * HEAD] = scaled[rows]
                stats = jnp.where(lane == head, level[rows], stats)
        put_stats(out_ref, stats)


def call(body, operands, columns, scalars, cost, name):
    row_count = operands[-1].shape[0]
    flops, loaded, transcendentals = cost
    return pl.pallas_call(
        body,
        out_shape=[jax.ShapeDtypeStruct((row_count, width), jnp.bfloat16) for width in columns],
        in_specs=[SMEM] * scalars + [VMEM] * (len(operands) - scalars),
        out_specs=[VMEM] * len(columns),
        compiler_params=pltpu.CompilerParams(vmem_limit_bytes=16 * 1024 * 1024),
        cost_estimate=pl.CostEstimate(
            flops=flops, bytes_accessed=loaded, transcendentals=transcendentals
        ),
        name=name,
    )(*operands)


def attend(loop, scalars, res_cache, mig_cache, queries, distance, name, forward=False, single=False, parts=(0, 1)):
    width = GROUP * HEAD
    query_counts = tuple(part.shape[1] // width for part in queries)
    packet_counts = tuple(PARTS[part][1] - PARTS[part][0] for part in parts)
    columns = [count * width + TILE for count in packet_counts]
    columns = ([sum(columns)] if single else columns) + [KV_HEADS * width] * forward
    pairs = queries[0].shape[0] * sum(query_counts) * GROUP * 2 * BLOCK
    return call(
        functools.partial(attend_body, loop, distance, (query_counts, packet_counts, forward, PARTS[parts[0]][0])),
        (*scalars, res_cache, mig_cache, *queries),
        columns,
        len(scalars),
        (pairs * HEAD * 4, 2 * 1024 * 1024, pairs),
        name,
    )


def join_packets(packets):
    stats = [get_stats(packet) for packet in packets]
    top = functools.reduce(jnp.maximum, stats)
    shares = [jnp.exp2(stat - top) for stat in stats]
    total = functools.reduce(jnp.add, shares)
    shares = [share / total for share in shares]
    heads = []
    for head in range(packet_heads(packets[0])):
        columns = slice(head * HEAD, (head + 1) * HEAD)
        terms = [
            packet[:, columns].astype(jnp.float32) * share[:, head : head + 1]
            for packet, share in zip(packets, shares, strict=True)
        ]
        heads.append(functools.reduce(jnp.add, terms))
    return heads, top + jnp.log2(total)


def put_heads(out_ref, first, heads):
    for head, joined in enumerate(heads, first):
        out_ref[:, head * HEAD : (head + 1) * HEAD] = joined.astype(jnp.bfloat16)


def join_body(*refs):
    count = len(refs) // 2
    ones, others, outs = refs[:count], refs[count : len(refs) - count], refs[len(refs) - count :]
    if len(others) < count:
        others = sections(others[0])
    for one_ref, other_ref, out_ref in zip(ones, others, outs, strict=True):
        heads, stats = join_packets((one_ref, other_ref))
        put_heads(out_ref, 0, heads)
        lane = lax.broadcasted_iota(jnp.int32, stats.shape, 1)
        put_stats(out_ref, jnp.where(lane < len(heads), stats, 0.0))


def join_part_body(own_ref, sum_ref, out_ref):
    put_heads(out_ref, 0, join_packets((own_ref, sum_ref))[0])


def join_home_body(done_ref, own_ref, sum_ref, out_ref):
    out_ref[:, : done_ref.shape[1]] = done_ref[...]
    put_heads(out_ref, done_ref.shape[1] // HEAD, join_packets((own_ref, sum_ref))[0])


def join(body, operands, columns, name):
    size = operands[0].shape[0] * sum(columns)
    return call(body, operands, columns, 0, (4 * size, 6 * size, 0), name)


def join_sums(ones, others, name):
    return join(join_body, (*ones, *others), [one.shape[1] for one in ones], name)


def join_home(own, sums):
    (part,) = join(join_part_body, (own[0], sums[0]), [own[0].shape[1] - TILE], "join_part")
    (whole,) = join(join_home_body, (part, own[1], sums[1]), [HEADS * HEAD], "join_home")
    return whole


def onward(value):
    sessions, loop = lax.axis_size("sess"), lax.axis_size("blk")
    pairs = [
        (s * loop + b, s * loop + (b + (-1 if s // 2 % 2 == 0 else 1)) % loop)
        for s in range(sessions)
        for b in range(loop)
    ]
    return lax.ppermute(value, ("sess", "blk"), pairs)


def per_device(queries, res_cache, mig_cache, res_ids, recv_ids, lengths):
    loop = lax.axis_size("blk")
    scalars = (res_ids, recv_ids, lengths)
    mine = queries[0]
    mine = tuple(
        mine[:, first * GROUP * HEAD : last * GROUP * HEAD] for first, last in PARTS
    )
    arrived = half_way(mig_cache)
    res_cache = load(res_cache)
    run = functools.partial(attend, loop, scalars, res_cache, arrived)
    before = tuple(onward(part) for part in mine)
    far_a, far_b = tuple(onward(part) for part in before)
    first_a, first_b = tuple(onward(part) for part in run(before, -1, "attend_before"))
    after_a = onward(far_a)
    part_far = run((far_a, far_b), -2, "attend_far")
    (sum_a,) = join_sums(part_far[:1], (first_a,), "join_far_a")
    second_a = onward(sum_a)
    far_b, sum_a = lax.optimization_barrier((far_b, sum_a))
    after_b = onward(far_b)
    (sum_b,) = join_sums(part_far[1:], (first_b,), "join_far_b")
    second_b = onward(sum_b)
    after_a, sum_b = lax.optimization_barrier((after_a, sum_b))
    (sum_a,) = join_sums(run((after_a,), 1, "attend_after_a", parts=(0,)), (second_a,), "join_after_a")
    third_a = onward(sum_a)
    after_b, sum_a = lax.optimization_barrier((after_b, sum_a))
    (sum_b,) = join_sums(run((after_b,), 1, "attend_after_b", parts=(1,)), (second_b,), "join_after_b")
    third_b = onward(sum_b)
    mine, third_a = lax.optimization_barrier((mine, third_a))
    own = run(mine, 0, "attend_own")
    return join_home(own, (third_a, third_b))[None]


def solution(mesh):
    placed = (
        P("sess", "blk", None),
        P(None, "sess", "blk", None),
        P(None, "sess", "blk", None),
        P("sess", "blk"),
        P("sess", "blk"),
        P("sess"),
    )
    return jax.shard_map(
        per_device, mesh=mesh, in_specs=placed, out_specs=P("sess", "blk", None), check_vma=False
    )
```

```python
import functools
import math

import jax
import jax.numpy as jnp
from jax import lax
from jax.experimental import pallas as pl
from jax.experimental.pallas import tpu as pltpu
from jax.sharding import PartitionSpec as P

HEADS = 64
KV_HEADS = 8
HEAD = 128
BLOCK = 256
QROWS = 64
GROUP = HEADS // KV_HEADS
TILE = 128
PARTS = ((0, KV_HEADS // 2), (KV_HEADS // 2, KV_HEADS))
FAR = -1e30
LOG2E = math.log2(math.e)

VMEM = pl.BlockSpec(memory_space=pltpu.VMEM)
SMEM = pl.BlockSpec(memory_space=pltpu.SMEM)


def half_way(value):
    count = lax.axis_size("sess")
    return lax.ppermute(value, "sess", [(s, (s + count // 2) % count) for s in range(count)])


def load_body(in_ref, out_ref, sem):
    copy = pltpu.make_async_copy(in_ref, out_ref, sem)
    copy.start()
    copy.wait()


def load(value):
    return pl.pallas_call(
        load_body,
        out_shape=jax.ShapeDtypeStruct(value.shape, value.dtype),
        in_specs=[pl.BlockSpec(memory_space=pl.ANY)],
        out_specs=VMEM,
        scratch_shapes=[pltpu.SemaphoreType.DMA],
        compiler_params=pltpu.CompilerParams(vmem_limit_bytes=16 * 1024 * 1024),
        cost_estimate=pl.CostEstimate(flops=10**11, bytes_accessed=2 * value.size * 2, transcendentals=0),
        name="load",
    )(value)


def split_three(value):
    high = value.astype(jnp.bfloat16)
    rest = value - high.astype(jnp.float32)
    middle = rest.astype(jnp.bfloat16)
    low = (rest - middle.astype(jnp.float32)).astype(jnp.bfloat16)
    return high, middle, low


def packet_heads(packet):
    return (packet.shape[1] - TILE) // HEAD


def put_stats(out_ref, stats):
    heads = packet_heads(out_ref)
    high, middle, low = (term.astype(jnp.float32) for term in split_three(stats))
    lane = lax.broadcasted_iota(jnp.int32, stats.shape, 1)
    middle = pltpu.roll(middle, heads, 1)
    low = pltpu.roll(low, 2 * heads, 1)
    tile = jnp.where(lane < heads, high, jnp.where(lane < 2 * heads, middle, low))
    out_ref[:, heads * HEAD :] = tile.astype(jnp.bfloat16)


def get_stats(packet_ref):
    heads = packet_heads(packet_ref)
    tile = packet_ref[:, heads * HEAD :].astype(jnp.float32)
    middle = pltpu.roll(tile, TILE - heads, 1)
    low = pltpu.roll(tile, TILE - 2 * heads, 1)
    return tile + middle + low


def sections(ref):
    width = GROUP * HEAD
    return [
        ref.at[:, first * width + part * TILE : last * width + (part + 1) * TILE]
        for part, (first, last) in enumerate(PARTS)
    ]


def attend_body(loop, distance, counts, res_id_ref, recv_id_ref, length_ref, res_ref, mig_ref, *refs):
    query_counts, packet_counts, forward, base = counts
    query_refs = refs[: len(query_counts)]
    out_refs = refs[len(query_counts) :]
    packet_refs = sections(out_refs[0]) if out_refs[0].shape[1] > HEADS * HEAD else out_refs
    row_count = query_refs[0].shape[0]
    way = 1 - 2 * lax.rem(lax.div(lax.axis_index("sess"), 2), 2)
    anchor = lax.rem(lax.axis_index("blk") + loop + distance * way, loop)
    start = length_ref[0] - QROWS + anchor * row_count
    row = lax.broadcasted_iota(jnp.int32, (row_count, BLOCK), 0)
    token = lax.broadcasted_iota(jnp.int32, (row_count, BLOCK), 1)
    bias = []
    for id_ref in (res_id_ref, recv_id_ref):
        limit = start - id_ref[0, 0] * BLOCK
        bias.append(jnp.where(token <= row + limit, 0.0, FAR).astype(jnp.float32))
    bias = jnp.concatenate(bias, axis=1)
    bias = jnp.concatenate([bias] * GROUP, axis=0)
    ones = jnp.ones((2 * BLOCK, HEAD), jnp.bfloat16)
    lane = lax.broadcasted_iota(jnp.int32, (row_count, TILE), 1)
    if forward:
        at = 0
        for query_ref in query_refs:
            out_refs[-1][:, at : at + query_ref.shape[1]] = query_ref[...]
            at += query_ref.shape[1]
    sources = [(ref, local) for ref, count in zip(query_refs, query_counts, strict=True) for local in range(count)]
    key_head = base
    for out_ref, count in zip(packet_refs, packet_counts):
        stats = jnp.zeros((row_count, TILE), jnp.float32)
        for local in range(count):
            query_ref, place = sources[key_head - base]
            columns = slice(key_head * HEAD, (key_head + 1) * HEAD)
            key_head += 1
            query = jnp.concatenate(
                [
                    query_ref[:, (place * GROUP + j) * HEAD : (place * GROUP + j + 1) * HEAD]
                    for j in range(GROUP)
                ],
                axis=0,
            )
            keys = jnp.concatenate([res_ref[0, 0, :, columns], mig_ref[0, 0, :, columns]], axis=0)
            values = jnp.concatenate([res_ref[1, 0, :, columns], mig_ref[1, 0, :, columns]], axis=0)
            scores = lax.dot_general(
                query, keys, (((1,), (1,)), ((), ())), preferred_element_type=jnp.float32
            )
            scores = scores * (LOG2E / math.sqrt(HEAD)) + bias
            row_max = jnp.max(scores, axis=1, keepdims=True)
            weights = jnp.exp2(scores - row_max).astype(jnp.bfloat16)
            mixed = jnp.dot(
                weights,
                jnp.concatenate([values, ones], axis=1),
                preferred_element_type=jnp.float32,
            )
            totals = mixed[:, HEAD:]
            scaled = (mixed[:, :HEAD] / totals).astype(jnp.bfloat16)
            level = row_max + jnp.log2(totals)
            for j in range(GROUP):
                head = local * GROUP + j
                rows = slice(j * row_count, (j + 1) * row_count)
                out_ref[:, head * HEAD : (head + 1) * HEAD] = scaled[rows]
                stats = jnp.where(lane == head, level[rows], stats)
        put_stats(out_ref, stats)


def call(body, operands, columns, scalars, cost, name):
    row_count = operands[-1].shape[0]
    flops, loaded, transcendentals = cost
    return pl.pallas_call(
        body,
        out_shape=[jax.ShapeDtypeStruct((row_count, width), jnp.bfloat16) for width in columns],
        in_specs=[SMEM] * scalars + [VMEM] * (len(operands) - scalars),
        out_specs=[VMEM] * len(columns),
        compiler_params=pltpu.CompilerParams(vmem_limit_bytes=16 * 1024 * 1024),
        cost_estimate=pl.CostEstimate(
            flops=flops, bytes_accessed=loaded, transcendentals=transcendentals
        ),
        name=name,
    )(*operands)


def attend(loop, scalars, res_cache, mig_cache, queries, distance, name, forward=False, single=False, parts=(0, 1)):
    width = GROUP * HEAD
    query_counts = tuple(part.shape[1] // width for part in queries)
    packet_counts = tuple(PARTS[part][1] - PARTS[part][0] for part in parts)
    columns = [count * width + TILE for count in packet_counts]
    columns = ([sum(columns)] if single else columns) + [KV_HEADS * width] * forward
    pairs = queries[0].shape[0] * sum(query_counts) * GROUP * 2 * BLOCK
    return call(
        functools.partial(attend_body, loop, distance, (query_counts, packet_counts, forward, PARTS[parts[0]][0])),
        (*scalars, res_cache, mig_cache, *queries),
        columns,
        len(scalars),
        (pairs * HEAD * 4, 2 * 1024 * 1024, pairs),
        name,
    )


def join_packets(packets):
    stats = [get_stats(packet) for packet in packets]
    top = functools.reduce(jnp.maximum, stats)
    shares = [jnp.exp2(stat - top) for stat in stats]
    total = functools.reduce(jnp.add, shares)
    shares = [share / total for share in shares]
    heads = []
    for head in range(packet_heads(packets[0])):
        columns = slice(head * HEAD, (head + 1) * HEAD)
        terms = [
            packet[:, columns].astype(jnp.float32) * share[:, head : head + 1]
            for packet, share in zip(packets, shares, strict=True)
        ]
        heads.append(functools.reduce(jnp.add, terms))
    return heads, top + jnp.log2(total)


def put_heads(out_ref, first, heads):
    for head, joined in enumerate(heads, first):
        out_ref[:, head * HEAD : (head + 1) * HEAD] = joined.astype(jnp.bfloat16)


def join_body(*refs):
    count = len(refs) // 2
    ones, others, outs = refs[:count], refs[count : len(refs) - count], refs[len(refs) - count :]
    if len(others) < count:
        others = sections(others[0])
    for one_ref, other_ref, out_ref in zip(ones, others, outs, strict=True):
        heads, stats = join_packets((one_ref, other_ref))
        put_heads(out_ref, 0, heads)
        lane = lax.broadcasted_iota(jnp.int32, stats.shape, 1)
        put_stats(out_ref, jnp.where(lane < len(heads), stats, 0.0))


def join_part_body(*refs):
    put_heads(refs[-1], 0, join_packets(refs[:-1])[0])


def join_home_body(done_ref, *refs):
    out_ref = refs[-1]
    out_ref[:, : done_ref.shape[1]] = done_ref[...]
    put_heads(out_ref, done_ref.shape[1] // HEAD, join_packets(refs[:-1])[0])


def join(body, operands, columns, name):
    size = operands[0].shape[0] * sum(columns)
    return call(body, operands, columns, 0, (4 * size, 6 * size, 0), name)


def join_sums(ones, others, name):
    return join(join_body, (*ones, *others), [one.shape[1] for one in ones], name)


def join_home(one, other):
    (part,) = join(join_part_body, one, [one[0].shape[1] - TILE], "join_part")
    (whole,) = join(join_home_body, (part, *other), [HEADS * HEAD], "join_home")
    return whole


def onward(value, steps=1):
    sessions, loop = lax.axis_size("sess"), lax.axis_size("blk")
    pairs = [
        (s * loop + b, s * loop + (b + (steps if s // 2 % 2 == 0 else -steps)) % loop)
        for s in range(sessions)
        for b in range(loop)
    ]
    return lax.ppermute(value, ("sess", "blk"), pairs)


def per_device(queries, res_cache, mig_cache, res_ids, recv_ids, lengths):
    loop = lax.axis_size("blk")
    scalars = (res_ids, recv_ids, lengths)
    mine = queries[0]
    whole = mine
    mine = tuple(
        mine[:, first * GROUP * HEAD : last * GROUP * HEAD] for first, last in PARTS
    )
    arrived = half_way(mig_cache)
    res_cache = load(res_cache)
    before = tuple(onward(part) for part in mine)
    far = tuple(onward(part) for part in before)
    whole, res_cache = lax.optimization_barrier((whole, res_cache))
    after = onward(whole, -1)
    run = functools.partial(attend, loop, scalars, res_cache, arrived)
    part_far = run(far, 2, "attend_far")
    via_a, via_b = tuple(onward(part) for part in part_far)
    *before, part_first = lax.optimization_barrier((*before, part_far[0]))
    part_before = run(before, -1, "attend_before")
    direct_a, direct_b = tuple(onward(part, -1) for part in part_before)
    after, part_last = lax.optimization_barrier((after, part_before[0]))
    part_after = run((after,), 1, "attend_after")
    (sum_a,) = join_sums(part_after[:1], (via_a,), "join_after_a")
    second_a = onward(sum_a)
    via_b, sum_a = lax.optimization_barrier((via_b, sum_a))
    (sum_b,) = join_sums(part_after[1:], (via_b,), "join_after_b")
    second_b = onward(sum_b)
    mine, second_a = lax.optimization_barrier((mine, second_a))
    own = run(mine, 0, "attend_own")
    return join_home((own[0], direct_a, second_a), (own[1], direct_b, second_b))[None]


def solution(mesh):
    placed = (
        P("sess", "blk", None),
        P(None, "sess", "blk", None),
        P(None, "sess", "blk", None),
        P("sess", "blk"),
        P("sess", "blk"),
        P("sess"),
    )
    return jax.shard_map(
        per_device, mesh=mesh, in_specs=placed, out_specs=P("sess", "blk", None), check_vma=False
    )
```

```python
import functools
import math

import jax
import jax.numpy as jnp
from jax import lax
from jax.experimental import pallas as pl
from jax.experimental.pallas import tpu as pltpu
from jax.sharding import PartitionSpec as P

HEADS = 64
KV_HEADS = 8
HEAD = 128
BLOCK = 256
QROWS = 64
GROUP = HEADS // KV_HEADS
TILE = 128
PARTS = ((0, KV_HEADS // 2), (KV_HEADS // 2, KV_HEADS))
FAR = -1e30
LOG2E = math.log2(math.e)

VMEM = pl.BlockSpec(memory_space=pltpu.VMEM)
SMEM = pl.BlockSpec(memory_space=pltpu.SMEM)


def half_way(value):
    count = lax.axis_size("sess")
    return lax.ppermute(value, "sess", [(s, (s + count // 2) % count) for s in range(count)])


def load_body(in_ref, out_ref, sem):
    copy = pltpu.make_async_copy(in_ref, out_ref, sem)
    copy.start()
    copy.wait()


def load(value):
    return pl.pallas_call(
        load_body,
        out_shape=jax.ShapeDtypeStruct(value.shape, value.dtype),
        in_specs=[pl.BlockSpec(memory_space=pl.ANY)],
        out_specs=VMEM,
        scratch_shapes=[pltpu.SemaphoreType.DMA],
        compiler_params=pltpu.CompilerParams(vmem_limit_bytes=16 * 1024 * 1024),
        cost_estimate=pl.CostEstimate(flops=10**11, bytes_accessed=2 * value.size * 2, transcendentals=0),
        name="load",
    )(value)


def split_three(value):
    high = value.astype(jnp.bfloat16)
    rest = value - high.astype(jnp.float32)
    middle = rest.astype(jnp.bfloat16)
    low = (rest - middle.astype(jnp.float32)).astype(jnp.bfloat16)
    return high, middle, low


def packet_heads(packet):
    return (packet.shape[1] - TILE) // HEAD


def put_stats(out_ref, stats):
    heads = packet_heads(out_ref)
    high, middle, low = (term.astype(jnp.float32) for term in split_three(stats))
    lane = lax.broadcasted_iota(jnp.int32, stats.shape, 1)
    middle = pltpu.roll(middle, heads, 1)
    low = pltpu.roll(low, 2 * heads, 1)
    tile = jnp.where(lane < heads, high, jnp.where(lane < 2 * heads, middle, low))
    out_ref[:, heads * HEAD :] = tile.astype(jnp.bfloat16)


def get_stats(packet_ref):
    heads = packet_heads(packet_ref)
    tile = packet_ref[:, heads * HEAD :].astype(jnp.float32)
    middle = pltpu.roll(tile, TILE - heads, 1)
    low = pltpu.roll(tile, TILE - 2 * heads, 1)
    return tile + middle + low


def sections(ref):
    width = GROUP * HEAD
    return [
        ref.at[:, first * width + part * TILE : last * width + (part + 1) * TILE]
        for part, (first, last) in enumerate(PARTS)
    ]


def attend_body(loop, distance, counts, res_id_ref, recv_id_ref, length_ref, res_ref, mig_ref, *refs):
    query_counts, packet_counts, forward, base = counts
    query_refs = refs[: len(query_counts)]
    out_refs = refs[len(query_counts) :]
    packet_refs = sections(out_refs[0]) if out_refs[0].shape[1] > HEADS * HEAD else out_refs
    row_count = query_refs[0].shape[0]
    way = 1 - 2 * lax.rem(lax.div(lax.axis_index("sess"), 2), 2)
    anchor = lax.rem(lax.axis_index("blk") + loop + distance * way, loop)
    start = length_ref[0] - QROWS + anchor * row_count
    row = lax.broadcasted_iota(jnp.int32, (row_count, BLOCK), 0)
    token = lax.broadcasted_iota(jnp.int32, (row_count, BLOCK), 1)
    bias = []
    for id_ref in (res_id_ref, recv_id_ref):
        limit = start - id_ref[0, 0] * BLOCK
        bias.append(jnp.where(token <= row + limit, 0.0, FAR).astype(jnp.float32))
    bias = jnp.concatenate(bias, axis=1)
    bias = jnp.concatenate([bias] * GROUP, axis=0)
    ones = jnp.ones((2 * BLOCK, HEAD), jnp.bfloat16)
    lane = lax.broadcasted_iota(jnp.int32, (row_count, TILE), 1)
    if forward:
        at = 0
        for query_ref in query_refs:
            out_refs[-1][:, at : at + query_ref.shape[1]] = query_ref[...]
            at += query_ref.shape[1]
    sources = [(ref, local) for ref, count in zip(query_refs, query_counts, strict=True) for local in range(count)]
    key_head = base
    for out_ref, count in zip(packet_refs, packet_counts):
        stats = jnp.zeros((row_count, TILE), jnp.float32)
        for local in range(count):
            query_ref, place = sources[key_head - base]
            columns = slice(key_head * HEAD, (key_head + 1) * HEAD)
            key_head += 1
            query = jnp.concatenate(
                [
                    query_ref[:, (place * GROUP + j) * HEAD : (place * GROUP + j + 1) * HEAD]
                    for j in range(GROUP)
                ],
                axis=0,
            )
            keys = jnp.concatenate([res_ref[0, 0, :, columns], mig_ref[0, 0, :, columns]], axis=0)
            values = jnp.concatenate([res_ref[1, 0, :, columns], mig_ref[1, 0, :, columns]], axis=0)
            scores = lax.dot_general(
                query, keys, (((1,), (1,)), ((), ())), preferred_element_type=jnp.float32
            )
            scores = scores * (LOG2E / math.sqrt(HEAD)) + bias
            row_max = jnp.max(scores, axis=1, keepdims=True)
            weights = jnp.exp2(scores - row_max).astype(jnp.bfloat16)
            mixed = jnp.dot(
                weights,
                jnp.concatenate([values, ones], axis=1),
                preferred_element_type=jnp.float32,
            )
            totals = mixed[:, HEAD:]
            scaled = (mixed[:, :HEAD] / totals).astype(jnp.bfloat16)
            level = row_max + jnp.log2(totals)
            for j in range(GROUP):
                head = local * GROUP + j
                rows = slice(j * row_count, (j + 1) * row_count)
                out_ref[:, head * HEAD : (head + 1) * HEAD] = scaled[rows]
                stats = jnp.where(lane == head, level[rows], stats)
        put_stats(out_ref, stats)


def call(body, operands, columns, scalars, cost, name):
    row_count = operands[-1].shape[0]
    flops, loaded, transcendentals = cost
    return pl.pallas_call(
        body,
        out_shape=[jax.ShapeDtypeStruct((row_count, width), jnp.bfloat16) for width in columns],
        in_specs=[SMEM] * scalars + [VMEM] * (len(operands) - scalars),
        out_specs=[VMEM] * len(columns),
        compiler_params=pltpu.CompilerParams(vmem_limit_bytes=16 * 1024 * 1024),
        cost_estimate=pl.CostEstimate(
            flops=flops, bytes_accessed=loaded, transcendentals=transcendentals
        ),
        name=name,
    )(*operands)


def attend(loop, scalars, res_cache, mig_cache, queries, distance, name, forward=False, single=False, parts=(0, 1)):
    width = GROUP * HEAD
    query_counts = tuple(part.shape[1] // width for part in queries)
    packet_counts = tuple(PARTS[part][1] - PARTS[part][0] for part in parts)
    columns = [count * width + TILE for count in packet_counts]
    columns = ([sum(columns)] if single else columns) + [KV_HEADS * width] * forward
    pairs = queries[0].shape[0] * sum(query_counts) * GROUP * 2 * BLOCK
    return call(
        functools.partial(attend_body, loop, distance, (query_counts, packet_counts, forward, PARTS[parts[0]][0])),
        (*scalars, res_cache, mig_cache, *queries),
        columns,
        len(scalars),
        (pairs * HEAD * 4, 2 * 1024 * 1024, pairs),
        name,
    )


def join_packets(packets):
    stats = [get_stats(packet) for packet in packets]
    top = functools.reduce(jnp.maximum, stats)
    shares = [jnp.exp2(stat - top) for stat in stats]
    total = functools.reduce(jnp.add, shares)
    shares = [share / total for share in shares]
    heads = []
    for head in range(packet_heads(packets[0])):
        columns = slice(head * HEAD, (head + 1) * HEAD)
        terms = [
            packet[:, columns].astype(jnp.float32) * share[:, head : head + 1]
            for packet, share in zip(packets, shares, strict=True)
        ]
        heads.append(functools.reduce(jnp.add, terms))
    return heads, top + jnp.log2(total)


def put_heads(out_ref, first, heads):
    for head, joined in enumerate(heads, first):
        out_ref[:, head * HEAD : (head + 1) * HEAD] = joined.astype(jnp.bfloat16)


def join_body(*refs):
    count = len(refs) // 2
    ones, others, outs = refs[:count], refs[count : len(refs) - count], refs[len(refs) - count :]
    if len(others) < count:
        others = sections(others[0])
    for one_ref, other_ref, out_ref in zip(ones, others, outs, strict=True):
        heads, stats = join_packets((one_ref, other_ref))
        put_heads(out_ref, 0, heads)
        lane = lax.broadcasted_iota(jnp.int32, stats.shape, 1)
        put_stats(out_ref, jnp.where(lane < len(heads), stats, 0.0))


def join_part_body(*refs):
    put_heads(refs[-1], 0, join_packets(refs[:-1])[0])


def join_home_body(done_ref, *refs):
    out_ref = refs[-1]
    out_ref[:, : done_ref.shape[1]] = done_ref[...]
    put_heads(out_ref, done_ref.shape[1] // HEAD, join_packets(refs[:-1])[0])


def join(body, operands, columns, name):
    size = operands[0].shape[0] * sum(columns)
    return call(body, operands, columns, 0, (4 * size, 6 * size, 0), name)


def join_sums(ones, others, name):
    return join(join_body, (*ones, *others), [one.shape[1] for one in ones], name)


def join_home(one, other):
    (part,) = join(join_part_body, one, [one[0].shape[1] - TILE], "join_part")
    (whole,) = join(join_home_body, (part, *other), [HEADS * HEAD], "join_home")
    return whole


def onward(value, steps=1):
    sessions, loop = lax.axis_size("sess"), lax.axis_size("blk")
    pairs = [
        (s * loop + b, s * loop + (b + (steps if s // 2 % 2 == 0 else -steps)) % loop)
        for s in range(sessions)
        for b in range(loop)
    ]
    return lax.ppermute(value, ("sess", "blk"), pairs)


def per_device(queries, res_cache, mig_cache, res_ids, recv_ids, lengths):
    loop = lax.axis_size("blk")
    scalars = (res_ids, recv_ids, lengths)
    mine = queries[0]
    whole = mine
    mine = tuple(
        mine[:, first * GROUP * HEAD : last * GROUP * HEAD] for first, last in PARTS
    )
    arrived = half_way(mig_cache)
    res_cache = load(res_cache)
    before = tuple(onward(part) for part in mine)
    far = tuple(onward(part) for part in before)
    whole, res_cache = lax.optimization_barrier((whole, res_cache))
    after = onward(whole, -1)
    run = functools.partial(attend, loop, scalars, res_cache, arrived)
    part_far = run(far, 2, "attend_far")
    via_a, via_b = tuple(onward(part) for part in part_far)
    *before, part_first = lax.optimization_barrier((*before, part_far[0]))
    part_before = run(before, -1, "attend_before")
    direct_a, direct_b = tuple(onward(part, -1) for part in part_before)
    after, part_last = lax.optimization_barrier((after, part_before[0]))
    part_after = run((after,), 1, "attend_after")
    (sum_a,) = join_sums(part_after[:1], (via_a,), "join_after_a")
    second_a = onward(sum_a)
    via_b, sum_a = lax.optimization_barrier((via_b, sum_a))
    (sum_b,) = join_sums(part_after[1:], (via_b,), "join_after_b")
    second_b = onward(sum_b)
    mine, second_a = lax.optimization_barrier((mine, second_a))
    own = run(mine, 0, "attend_own")
    near = [join_sums(own[i : i + 1], (direct,), "join_near")[0] for i, direct in enumerate((direct_a, direct_b))]
    return join_home((near[0], second_a), (near[1], second_b))[None]


def solution(mesh):
    placed = (
        P("sess", "blk", None),
        P(None, "sess", "blk", None),
        P(None, "sess", "blk", None),
        P("sess", "blk"),
        P("sess", "blk"),
        P("sess"),
    )
    return jax.shard_map(
        per_device, mesh=mesh, in_specs=placed, out_specs=P("sess", "blk", None), check_vma=False
    )
```
